32 devices in a mesh: gx: 4 (over y, x), gz: 2 (over core), gy: 4 (over z).
Axes of the slice: x: 2, y: 2, z: 4, core: 2. Of those that a mesh axis runs over, the one named last changes fastest.
Arguments:
- fields: bfloat16 [1, 256, 1024, 2048], P(None, 'gy', 'gz', 'gx'), may hold values from -6 to 6
- conductance: float32 [257], replicated, may hold values from 0.5 to 2
- metric: float32 [256], replicated, may hold values from 0.5 to 2
- section_shift: float32 [256], replicated, may hold values from 0.002 to 0.02
- curvature: float32 [256], replicated, may hold values from 0.005 to 0.05
- damping: float32 [1], replicated, may hold values from 0.002 to 0.02
Outputs:
- adjoint_modes: float32 [1, 256, 512, 1024], P(None, 'gy', ('gx', 'gz'))
The draws below stay inside these ranges and needn't reach their ends.
All inputs are finite; a program needn't handle non-finite values.
Results may differ from the reference program's by a relative error of at most 0.0003.
Values may be sent and summed in bfloat16 or wider, within the bound.
A program may use at most 256 MiB of HBM per device.

```python
import math
import jax
import jax.numpy as jnp
from jax import lax

C = 1
NX = 2048
NZ = 1024
NY = 256
KX = 512
KZ = 512


def block_levels(own_key, extent, split, smallest, high):
    factor_of = 1.0
    for position, blocks in split:
        steps = jax.random.uniform(jax.random.fold_in(jax.random.fold_in(own_key, 6), position), (blocks,), jnp.float32, smallest / len(split), high / len(split))
        factor_of = factor_of * jnp.repeat(jnp.exp(steps), extent[position] // blocks).reshape((-1,) + (1,) * (len(extent) - 1 - position))
    return factor_of


def bell_draw(key, shape, spread, limit, pieces=(), kind=jnp.bfloat16):
    level = block_levels(key, shape, pieces, -0.22, 0.18) if pieces else 1.0
    entries = jax.random.normal(key, shape, jnp.float32) * spread * level
    return jnp.minimum(jnp.maximum(entries, -limit), limit).astype(kind)


def setup_inputs(seed: int = 0) -> dict:
    key_of = jax.random.split(jax.random.key(seed), 7)
    fields = bell_draw(key_of[0], (C, NY, NZ, NX), 1.0, 6.0, ((1, 4), (2, 2), (3, 4)))
    conductance = jnp.clip(jnp.exp(jax.random.uniform(key_of[1], (NY + 1,), jnp.float32, math.log(0.5), math.log(2.0))), 0.5, 2.0)
    metric = jnp.clip(jnp.exp(jax.random.uniform(key_of[2], (NY,), jnp.float32, math.log(0.5), math.log(2.0))), 0.5, 2.0)
    section_shift = jnp.clip(jnp.exp(jax.random.uniform(key_of[3], (NY,), jnp.float32, math.log(0.002), math.log(0.02))), 0.002, 0.02)
    curvature = jnp.clip(jnp.exp(jax.random.uniform(key_of[4], (NY,), jnp.float32, math.log(0.005), math.log(0.05))), 0.005, 0.05)
    damping = jnp.clip(jnp.exp(jax.random.uniform(key_of[5], (C,), jnp.float32, math.log(0.002), math.log(0.02))), 0.002, 0.02)
    return {"fields": fields, "conductance": conductance, "metric": metric, "section_shift": section_shift, "curvature": curvature, "damping": damping}


def wave_square(along_first, along_local, along_total, across_total):
    along = (along_first + jnp.arange(along_local, dtype=jnp.int32)).astype(jnp.float32) / along_total
    index = jnp.arange(2 * across_total, dtype=jnp.int32) % across_total
    signed = jnp.where(index < across_total // 2, index, index - across_total)
    across = signed.astype(jnp.float32) / (across_total // 2)
    return along[:, None] * along[:, None] + across[None, :] * across[None, :]

def thomas(lower_band, diagonal, upper_band, source):
    nought = jnp.zeros(source.shape[1:], jnp.float32)

    def forward(carry, entry):
        ratios, forward_swept = carry
        sub_coef, mid_coef, sup_coef, source_row = entry
        pivots = mid_coef - sub_coef * ratios
        ratios = sup_coef / pivots
        forward_swept = (source_row - sub_coef * forward_swept) / pivots
        return ((ratios, forward_swept), (ratios, forward_swept))
    unused, sweeps = lax.scan(forward, (nought, nought), (lower_band, diagonal, upper_band, source))

    def backward(solved, entry):
        ratios, forward_swept = entry
        solved = forward_swept - ratios * solved
        return (solved, solved)
    unused_last, values = lax.scan(backward, nought, sweeps, reverse=True)
    return values

def reference(fields, conductance, metric, section_shift, curvature, damping):
    pivot_scale = 1.0 / math.sqrt(NX * NZ)
    nought = jnp.zeros((1,), jnp.float32)
    padded = jnp.concatenate([nought, metric, nought])
    lower_band = -padded[:NY] * conductance[:NY]
    upper_band = -padded[2:] * conductance[1:]
    diag_base = metric * (conductance[:NY] + conductance[1:]) + section_shift
    square = wave_square(0, KX, KX, KZ)
    results = []
    for component in range(C):
        values = fields[component].astype(jnp.float32)
        along = jnp.fft.rfft(values, axis=2)[:, :, :KX]
        both = jnp.fft.fft(along, axis=1)
        kept = jnp.concatenate([both[:, :KZ // 2], both[:, NZ - KZ // 2:]], axis=1) * pivot_scale
        kept = jnp.transpose(kept, (0, 2, 1))
        source = jnp.concatenate([jnp.real(kept), jnp.imag(kept)], axis=2).astype(jnp.float32)
        diagonal = diag_base[:, None, None] + damping[component] + curvature[:, None, None] * square[None]
        results.append(thomas(lower_band, diagonal, upper_band, source))
    return jnp.stack(results)
```

```python
import functools
import math

import jax
import jax.numpy as jnp
import ml_dtypes
import numpy as np
from jax import lax
from jax.experimental import pallas as pl
from jax.experimental.pallas import tpu as pltpu
from jax.sharding import PartitionSpec as P

GROUP = ("gx", "gz")
CHUNKS = 4
MIB = 1024 * 1024


def two_pieces(matrix):
    high = matrix.astype(ml_dtypes.bfloat16)
    low = (matrix - high.astype(np.float64)).astype(ml_dtypes.bfloat16)
    return high, low


def across_matrix(length):
    total = length // 2
    index = np.arange(total)
    signed = np.where(index < total // 2, index, index - total)
    angle = (signed[:, None] * np.arange(length)[None, :] % length) * (2.0 * math.pi / length)
    return np.concatenate([np.cos(angle), -np.sin(angle)]) / math.sqrt(length)


def along_matrix(length):
    numbers = np.arange(length // 4)
    angle = (numbers[:, None] * np.arange(length)[None, :] % length) * (2.0 * math.pi / length)
    return np.concatenate([np.cos(angle), -np.sin(angle)]) / math.sqrt(length)


def wave_square(along_first, along_local, along_total, across_total):
    along = (along_first + jnp.arange(along_local, dtype=jnp.int32)).astype(
        jnp.float32
    ) / along_total
    index = jnp.arange(across_total, dtype=jnp.int32)
    signed = jnp.where(index < across_total // 2, index, index - across_total)
    across = signed.astype(jnp.float32) / (across_total // 2)
    return along[:, None] * along[:, None] + across[None, :] * across[None, :]


def dot(a, b):
    return lax.dot_general(a, b, (((1,), (0,)), ((), ())), preferred_element_type=jnp.float32)


def dot_nt(a, b):
    return lax.dot_general(a, b, (((1,), (1,)), ((), ())), preferred_element_type=jnp.float32)


def transform_kernel(gx, gz, data, zh, zl, xh, xl, out, gh, gl):
    z_local, x_local = data.shape[2], data.shape[3]
    modes = zh.shape[0]
    half = modes // 2
    kx_total = xh.shape[0] // 2
    joint = out.shape[0]
    step = min(256, modes)
    for block in range(gx):
        for first in range(0, modes, step):
            total = None
            for side in range(gz):
                piece = data[block * gz + side, 0]
                cols = slice(side * z_local, (side + 1) * z_local)
                rows = slice(first, first + step)
                term = dot(zh[rows, cols], piece) + dot(zl[rows, cols], piece)
                total = term if total is None else total + term
            high = total.astype(jnp.bfloat16)
            place = slice(block * x_local, (block + 1) * x_local)
            gh[first : first + step, place] = high
            gl[first : first + step, place] = (total - high.astype(jnp.float32)).astype(
                jnp.bfloat16
            )
    tile = 128
    width = 256
    per_dest = out.shape[2]
    for first in range(0, kx_total, tile):
        for col in range(0, half, width):
            def product(base, mode):
                rows = slice(base, base + tile)
                cols = slice(mode, mode + width)
                return (
                    dot_nt(xh[rows], gh[cols])
                    + dot_nt(xh[rows], gl[cols])
                    + dot_nt(xl[rows], gh[cols])
                )

            real = product(first, col) - product(kx_total + first, half + col)
            imag = product(kx_total + first, col) + product(first, half + col)
            for part in range(0, tile, min(tile, per_dest)):
                size = min(tile, per_dest)
                dest, at = divmod(first + part, per_dest)
                out[dest, 0, at : at + size, col : col + width] = real[part : part + size]
                out[dest, 0, at : at + size, half + col : half + col + width] = imag[
                    part : part + size
                ]
    del joint


def transform(data, pieces, gx, gz):
    groups, rows, z_local, x_local = data.shape
    zh, zl, xh, xl = pieces
    modes = zh.shape[0]
    kx_total = xh.shape[0] // 2
    along_length = xh.shape[1]
    whole = lambda a: pl.BlockSpec(a.shape, lambda r: (0, 0), pipeline_mode=pl.Buffered(1))
    return pl.pallas_call(
        functools.partial(transform_kernel, gx, gz),
        grid=(rows,),
        in_specs=[
            pl.BlockSpec((groups, 1, z_local, x_local), lambda r: (0, r, 0, 0)),
            whole(zh), whole(zl), whole(xh), whole(xl),
        ],
        out_specs=pl.BlockSpec((groups, 1, kx_total // groups, modes), lambda r: (0, r, 0, 0)),
        out_shape=jax.ShapeDtypeStruct(
            (groups, rows, kx_total // groups, modes), jnp.float32
        ),
        scratch_shapes=[pltpu.VMEM((modes, along_length), jnp.bfloat16)] * 2,
        compiler_params=pltpu.CompilerParams(vmem_limit_bytes=56 * MIB),
        cost_estimate=pl.CostEstimate(
            flops=2 * rows * (2 * modes * along_length * gz * z_local
                              + 3 * 2 * kx_total * along_length * modes),
            bytes_accessed=data.size * 2 + 4 * rows * kx_total * modes,
            transcendentals=0,
        ),
        name="transform",
    )(data, zh, zl, xh, xl)


def spike_kernel(low, up, diag, curve, square, ip_ref, g_ref, h_ref, edge_ref):
    rows = ip_ref.shape[0]
    sq = square[...]
    zero = jnp.zeros_like(sq)

    def ahead(i, carry):
        ratio, spike = carry
        inverse = 1.0 / (diag[i] + curve[i] * sq - low[i] * ratio)
        spike = -low[i] * spike * inverse
        ip_ref[i] = inverse
        g_ref[i] = spike
        return up[i] * inverse, spike

    lax.fori_loop(0, rows, ahead, (zero, zero - 1.0), unroll=4)

    def back(n, carry):
        i = rows - 1 - n
        g_next, h_next = carry
        ratio = up[i] * ip_ref[i]
        g = g_ref[i] - ratio * g_next
        h = -ratio * h_next
        g_ref[i] = g
        h_ref[i] = h
        return g, h

    lax.fori_loop(0, rows, back, (zero, zero - 1.0), unroll=4)
    edge_ref[0] = g_ref[0]
    edge_ref[1] = g_ref[rows - 1]
    edge_ref[2] = h_ref[0]
    edge_ref[3] = h_ref[rows - 1]


def sweep_kernel(chunks, low, up, ip_ref, *refs):
    sources, (w_ref, edge_ref) = refs[:chunks], refs[chunks:]
    rows, width, modes = w_ref.shape
    half = modes // 2
    senders, per_chunk = sources[0].shape[0], sources[0].shape[1]
    per_sender = rows // senders
    zero = jnp.zeros((width, half), jnp.float32)

    def ahead(sender, carry):
        real, imag = carry
        for within in range(per_sender):
            i = sender * per_sender + within
            source = sources[within // per_chunk]
            inner = within % per_chunk
            inverse = ip_ref[i]
            real = (source[sender, inner, :, :half] - low[i] * real) * inverse
            imag = (source[sender, inner, :, half:] - low[i] * imag) * inverse
            w_ref[i, :, :half] = real
            w_ref[i, :, half:] = imag
        return real, imag

    lax.fori_loop(0, senders, ahead, (zero, zero))

    def back(n, carry):
        real, imag = carry
        i = rows - 1 - n
        ratio = up[i] * ip_ref[i]
        real = w_ref[i, :, :half] - ratio * real
        imag = w_ref[i, :, half:] - ratio * imag
        w_ref[i, :, :half] = real
        w_ref[i, :, half:] = imag
        return real, imag

    lax.fori_loop(0, rows, back, (zero, zero), unroll=8)
    edge_ref[0] = w_ref[0]
    edge_ref[1] = w_ref[rows - 1]


def finish_kernel(count, place, w_ref, g_ref, h_ref, edges, spikes, out):
    rows, width, modes = w_ref.shape
    half = modes // 2
    zero = jnp.zeros((width, half), jnp.float32)
    me = place[0]
    joined = []
    for side in range(2):
        cols = slice(side * half, (side + 1) * half)
        p, q = zero, zero
        kept = []
        for k in range(count):
            wa, wz = edges[k, 0, :, cols], edges[k, 1, :, cols]
            ga, gz, ha, hz = (spikes[k, n] for n in range(4))
            scale = 1.0 / (1.0 - ga * q)
            r = (wa - ga * p) * scale
            s = ha * scale
            p, q = wz - gz * p + gz * q * r, gz * q * s + hz
            kept.append((r, s, p, q))
        before, after = zero, zero
        following = zero
        for k in range(count - 1, -1, -1):
            r, s, p, q = kept[k]
            first = r - s * following
            last = p - q * following
            after = jnp.where(me == k - 1, first, after)
            before = jnp.where(me == k + 1, last, before)
            following = first
        joined.append((before, after))

    def one(i, carry):
        g, h = g_ref[i], h_ref[i]
        for side in range(2):
            cols = slice(side * half, (side + 1) * half)
            before, after = joined[side]
            out[0, i, :, cols] = w_ref[i, :, cols] - g * before - h * after
        return carry

    lax.fori_loop(0, rows, one, 0, unroll=4)


def local(pieces, fields, conductance, metric, section_shift, curvature, damping):
    row_count, z_local, x_local = fields.shape[1:]
    gx, gz, gy = (lax.axis_size(a) for a in ("gx", "gz", "gy"))
    groups = gx * gz
    my_group = lax.axis_index("gy")
    along_total = gx * x_local // 4
    along_local = along_total // groups
    across_total = gz * z_local // 2
    modes = 2 * across_total
    per_sender = row_count // groups
    chunks = min(CHUNKS, per_sender)
    per_chunk = per_sender // chunks

    raw = fields.reshape(groups, per_sender, z_local, x_local)
    sources = []
    for chunk in range(chunks):
        part = raw[:, chunk * per_chunk : (chunk + 1) * per_chunk]
        lines = lax.all_to_all(part, GROUP, split_axis=0, concat_axis=0)
        spectra = transform(lines, pieces, gx, gz)
        sources.append(lax.all_to_all(spectra, GROUP, split_axis=0, concat_axis=0))

    joint_index = lax.axis_index("gx") * gz + lax.axis_index("gz")
    square = wave_square(joint_index * along_local, along_local, along_total, across_total)
    nought = jnp.zeros((1,), jnp.float32)
    first_row = my_group * row_count
    metric_pad = jnp.concatenate([nought, metric, nought])
    metric_rows = lax.dynamic_slice_in_dim(metric_pad, first_row, row_count + 2)
    face_rows = lax.dynamic_slice_in_dim(conductance, first_row, row_count + 1)
    shift_rows = lax.dynamic_slice_in_dim(section_shift, first_row, row_count)
    curve_rows = lax.dynamic_slice_in_dim(curvature, first_row, row_count)
    low = -metric_rows[:row_count] * face_rows[:row_count]
    up = -metric_rows[2:] * face_rows[1:]
    diag = (
        metric_rows[1 : row_count + 1] * (face_rows[:row_count] + face_rows[1:])
        + shift_rows
        + damping[0]
    )
    smem = pl.BlockSpec(memory_space=pltpu.SMEM)
    params = pltpu.CompilerParams(vmem_limit_bytes=48 * MIB)

    block = min(16, along_local)
    row_shape = jax.ShapeDtypeStruct((row_count, along_local, across_total), jnp.float32)
    row_spec = pl.BlockSpec((row_count, block, across_total), lambda n: (0, n, 0))
    inverse, g_rows, h_rows, spikes = pl.pallas_call(
        spike_kernel,
        grid=(along_local // block,),
        in_specs=[smem] * 4 + [pl.BlockSpec((block, across_total), lambda n: (n, 0))],
        out_specs=[row_spec] * 3
        + [pl.BlockSpec((4, block, across_total), lambda n: (0, n, 0))],
        out_shape=[row_shape] * 3
        + [jax.ShapeDtypeStruct((4, along_local, across_total), jnp.float32)],
        compiler_params=params,
        cost_estimate=pl.CostEstimate(
            flops=12 * row_count * along_local * across_total,
            bytes_accessed=60 * MIB,
            transcendentals=0,
        ),
        name="spikes",
    )(low, up, diag, curve_rows, square)
    all_spikes = lax.all_gather(spikes, "gy")

    block = min(8, along_local)
    full_spec = pl.BlockSpec((row_count, block, modes), lambda n: (0, n, 0))
    half_spec = pl.BlockSpec((row_count, block, across_total), lambda n: (0, n, 0))
    swept, edges = pl.pallas_call(
        functools.partial(sweep_kernel, chunks),
        grid=(along_local // block,),
        in_specs=[smem] * 2
        + [half_spec]
        + [pl.BlockSpec((groups, per_chunk, block, modes), lambda n: (0, 0, n, 0))] * chunks,
        out_specs=[full_spec, pl.BlockSpec((2, block, modes), lambda n: (0, n, 0))],
        out_shape=[
            jax.ShapeDtypeStruct((row_count, along_local, modes), jnp.float32),
            jax.ShapeDtypeStruct((2, along_local, modes), jnp.float32),
        ],
        compiler_params=params,
        name="sweep",
    )(low, up, inverse, *sources)
    all_edges = lax.all_gather(edges, "gy")
    return pl.pallas_call(
        functools.partial(finish_kernel, gy),
        grid=(along_local // block,),
        in_specs=[
            smem, full_spec, half_spec, half_spec,
            pl.BlockSpec((gy, 2, block, modes), lambda n: (0, 0, n, 0)),
            pl.BlockSpec((gy, 4, block, across_total), lambda n: (0, 0, n, 0)),
        ],
        out_specs=pl.BlockSpec((1, row_count, block, modes), lambda n: (0, 0, n, 0)),
        out_shape=jax.ShapeDtypeStruct((1, row_count, along_local, modes), jnp.float32),
        compiler_params=params,
        name="finish",
    )(jnp.reshape(my_group, (1,)).astype(jnp.int32), swept, g_rows, h_rows, all_edges, all_spikes)


def solution(mesh):
    placed = (P(None, "gy", "gz", "gx"), P(), P(), P(), P(), P())

    def run(fields, *rest):
        pieces = two_pieces(across_matrix(fields.shape[2])) + two_pieces(
            along_matrix(fields.shape[3])
        )
        pieces = tuple(jnp.asarray(a) for a in pieces)
        return jax.shard_map(
            local,
            mesh=mesh,
            in_specs=((P(),) * 4,) + placed,
            out_specs=P(None, "gy", ("gx", "gz"), None),
            check_vma=False,
        )(pieces, fields, *rest)

    return run
```

```python
import functools
import math

import jax
import jax.numpy as jnp
import ml_dtypes
import numpy as np
from jax import lax
from jax.experimental import pallas as pl
from jax.experimental.pallas import tpu as pltpu
from jax.sharding import PartitionSpec as P

GROUP = ("gx", "gz")
CHUNKS = 4
MIB = 1024 * 1024


def two_pieces(matrix):
    high = matrix.astype(ml_dtypes.bfloat16)
    low = (matrix - high.astype(np.float64)).astype(ml_dtypes.bfloat16)
    return high, low


def across_matrix(length):
    total = length // 2
    index = np.arange(total)
    signed = np.where(index < total // 2, index, index - total)
    angle = (signed[:, None] * np.arange(length)[None, :] % length) * (2.0 * math.pi / length)
    return np.concatenate([np.cos(angle), -np.sin(angle)]) / math.sqrt(length)


def along_matrix(length):
    numbers = np.arange(length // 4)
    angle = (numbers[:, None] * np.arange(length)[None, :] % length) * (2.0 * math.pi / length)
    return np.concatenate([np.cos(angle), -np.sin(angle)]) / math.sqrt(length)


def wave_square(along_first, along_local, along_total, across_total):
    along = (along_first + jnp.arange(along_local, dtype=jnp.int32)).astype(
        jnp.float32
    ) / along_total
    index = jnp.arange(across_total, dtype=jnp.int32)
    signed = jnp.where(index < across_total // 2, index, index - across_total)
    across = signed.astype(jnp.float32) / (across_total // 2)
    return along[:, None] * along[:, None] + across[None, :] * across[None, :]


def dot(a, b):
    return lax.dot_general(a, b, (((1,), (0,)), ((), ())), preferred_element_type=jnp.float32)


def dot_nt(a, b):
    return lax.dot_general(a, b, (((1,), (1,)), ((), ())), preferred_element_type=jnp.float32)


def transform_kernel(gx, gz, data, zh, zl, xh, xl, out, gh, gl):
    z_local, x_local = data.shape[2], data.shape[3]
    modes = zh.shape[0]
    half = modes // 2
    kx_total = xh.shape[0] // 2
    joint = out.shape[0]
    step = min(256, modes)
    for block in range(gx):
        for first in range(0, modes, step):
            total = None
            for side in range(gz):
                piece = data[block * gz + side, 0]
                cols = slice(side * z_local, (side + 1) * z_local)
                rows = slice(first, first + step)
                term = dot(zh[rows, cols], piece) + dot(zl[rows, cols], piece)
                total = term if total is None else total + term
            high = total.astype(jnp.bfloat16)
            place = slice(block * x_local, (block + 1) * x_local)
            gh[first : first + step, place] = high
            gl[first : first + step, place] = (total - high.astype(jnp.float32)).astype(
                jnp.bfloat16
            )
    tile = 128
    width = 256
    per_dest = out.shape[2]
    for first in range(0, kx_total, tile):
        for col in range(0, half, width):
            def product(base, mode):
                rows = slice(base, base + tile)
                cols = slice(mode, mode + width)
                return (
                    dot_nt(xh[rows], gh[cols])
                    + dot_nt(xh[rows], gl[cols])
                    + dot_nt(xl[rows], gh[cols])
                )

            real = product(first, col) - product(kx_total + first, half + col)
            imag = product(kx_total + first, col) + product(first, half + col)
            for part in range(0, tile, min(tile, per_dest)):
                size = min(tile, per_dest)
                dest, at = divmod(first + part, per_dest)
                out[dest, 0, at : at + size, col : col + width] = real[part : part + size]
                out[dest, 0, at : at + size, half + col : half + col + width] = imag[
                    part : part + size
                ]
    del joint


def transform(data, pieces, gx, gz):
    groups, rows, z_local, x_local = data.shape
    zh, zl, xh, xl = pieces
    modes = zh.shape[0]
    kx_total = xh.shape[0] // 2
    along_length = xh.shape[1]
    whole = lambda a: pl.BlockSpec(a.shape, lambda r: (0, 0), pipeline_mode=pl.Buffered(1))
    return pl.pallas_call(
        functools.partial(transform_kernel, gx, gz),
        grid=(rows,),
        in_specs=[
            pl.BlockSpec((groups, 1, z_local, x_local), lambda r: (0, r, 0, 0)),
            whole(zh), whole(zl), whole(xh), whole(xl),
        ],
        out_specs=pl.BlockSpec((groups, 1, kx_total // groups, modes), lambda r: (0, r, 0, 0)),
        out_shape=jax.ShapeDtypeStruct(
            (groups, rows, kx_total // groups, modes), jnp.float32
        ),
        scratch_shapes=[pltpu.VMEM((modes, along_length), jnp.bfloat16)] * 2,
        compiler_params=pltpu.CompilerParams(vmem_limit_bytes=56 * MIB),
        cost_estimate=pl.CostEstimate(
            flops=2 * rows * (2 * modes * along_length * gz * z_local
                              + 3 * 2 * kx_total * along_length * modes),
            bytes_accessed=data.size * 2 + 4 * rows * kx_total * modes,
            transcendentals=0,
        ),
        name="transform",
    )(data, zh, zl, xh, xl)


def spike_kernel(low, up, diag, curve, square, ip_ref, g_ref, h_ref, edge_ref):
    rows = ip_ref.shape[0]
    sq = square[...]
    zero = jnp.zeros_like(sq)

    def ahead(i, carry):
        ratio, spike = carry
        inverse = 1.0 / (diag[i] + curve[i] * sq - low[i] * ratio)
        spike = -low[i] * spike * inverse
        ip_ref[i] = inverse
        g_ref[i] = spike
        return up[i] * inverse, spike

    lax.fori_loop(0, rows, ahead, (zero, zero - 1.0), unroll=4)

    def back(n, carry):
        i = rows - 1 - n
        g_next, h_next = carry
        ratio = up[i] * ip_ref[i]
        g = g_ref[i] - ratio * g_next
        h = -ratio * h_next
        g_ref[i] = g
        h_ref[i] = h
        return g, h

    lax.fori_loop(0, rows, back, (zero, zero - 1.0), unroll=4)
    edge_ref[0] = g_ref[0]
    edge_ref[1] = g_ref[rows - 1]
    edge_ref[2] = h_ref[0]
    edge_ref[3] = h_ref[rows - 1]


def sweep_kernel(chunks, low, up, ip_ref, *refs):
    sources, (w_ref, edge_ref) = refs[:chunks], refs[chunks:]
    rows, width, modes = w_ref.shape
    half = modes // 2
    senders, per_chunk = sources[0].shape[0], sources[0].shape[1]
    per_sender = rows // senders
    zero = jnp.zeros((width, half), jnp.float32)

    def ahead(sender, carry):
        real, imag = carry
        for within in range(per_sender):
            i = sender * per_sender + within
            source = sources[within // per_chunk]
            inner = within % per_chunk
            inverse = ip_ref[i]
            real = (source[sender, inner, :, :half] - low[i] * real) * inverse
            imag = (source[sender, inner, :, half:] - low[i] * imag) * inverse
            w_ref[i, :, :half] = real
            w_ref[i, :, half:] = imag
        return real, imag

    lax.fori_loop(0, senders, ahead, (zero, zero))

    def back(n, carry):
        real, imag = carry
        i = rows - 1 - n
        ratio = up[i] * ip_ref[i]
        real = w_ref[i, :, :half] - ratio * real
        imag = w_ref[i, :, half:] - ratio * imag
        w_ref[i, :, :half] = real
        w_ref[i, :, half:] = imag
        return real, imag

    lax.fori_loop(0, rows, back, (zero, zero), unroll=8)
    edge_ref[0] = w_ref[0]
    edge_ref[1] = w_ref[rows - 1]


def finish_kernel(count, place, w_ref, g_ref, h_ref, edges, spikes, out):
    rows, width, modes = w_ref.shape
    half = modes // 2
    zero = jnp.zeros((width, half), jnp.float32)
    me = place[0]
    joined = []
    for side in range(2):
        cols = slice(side * half, (side + 1) * half)
        p, q = zero, zero
        kept = []
        for k in range(count):
            wa, wz = edges[k, 0, :, cols], edges[k, 1, :, cols]
            ga, gz, ha, hz = (spikes[k, n] for n in range(4))
            scale = 1.0 / (1.0 - ga * q)
            r = (wa - ga * p) * scale
            s = ha * scale
            p, q = wz - gz * p + gz * q * r, gz * q * s + hz
            kept.append((r, s, p, q))
        before, after = zero, zero
        following = zero
        for k in range(count - 1, -1, -1):
            r, s, p, q = kept[k]
            first = r - s * following
            last = p - q * following
            after = jnp.where(me == k - 1, first, after)
            before = jnp.where(me == k + 1, last, before)
            following = first
        joined.append((before, after))

    def one(i, carry):
        g, h = g_ref[i], h_ref[i]
        for side in range(2):
            cols = slice(side * half, (side + 1) * half)
            before, after = joined[side]
            out[0, i, :, cols] = w_ref[i, :, cols] - g * before - h * after
        return carry

    lax.fori_loop(0, rows, one, 0, unroll=4)


def local(pieces, fields, conductance, metric, section_shift, curvature, damping):
    row_count, z_local, x_local = fields.shape[1:]
    gx, gz, gy = (lax.axis_size(a) for a in ("gx", "gz", "gy"))
    groups = gx * gz
    my_group = lax.axis_index("gy")
    along_total = gx * x_local // 4
    along_local = along_total // groups
    across_total = gz * z_local // 2
    modes = 2 * across_total
    per_sender = row_count // groups
    chunks = min(CHUNKS, per_sender)
    per_chunk = per_sender // chunks

    raw = fields.reshape(groups, per_sender, z_local, x_local)
    sources, done = [], []
    for chunk in range(chunks):
        part = raw[:, chunk * per_chunk : (chunk + 1) * per_chunk]
        if chunk >= 2:
            part, done[chunk - 2] = lax.optimization_barrier((part, done[chunk - 2]))
        lines = lax.all_to_all(part, GROUP, split_axis=0, concat_axis=0)
        done.append(transform(lines, pieces, gx, gz))
    for spectra in done:
        sources.append(lax.all_to_all(spectra, GROUP, split_axis=0, concat_axis=0))

    joint_index = lax.axis_index("gx") * gz + lax.axis_index("gz")
    square = wave_square(joint_index * along_local, along_local, along_total, across_total)
    nought = jnp.zeros((1,), jnp.float32)
    first_row = my_group * row_count
    metric_pad = jnp.concatenate([nought, metric, nought])
    metric_rows = lax.dynamic_slice_in_dim(metric_pad, first_row, row_count + 2)
    face_rows = lax.dynamic_slice_in_dim(conductance, first_row, row_count + 1)
    shift_rows = lax.dynamic_slice_in_dim(section_shift, first_row, row_count)
    curve_rows = lax.dynamic_slice_in_dim(curvature, first_row, row_count)
    low = -metric_rows[:row_count] * face_rows[:row_count]
    up = -metric_rows[2:] * face_rows[1:]
    diag = (
        metric_rows[1 : row_count + 1] * (face_rows[:row_count] + face_rows[1:])
        + shift_rows
        + damping[0]
    )
    smem = pl.BlockSpec(memory_space=pltpu.SMEM)
    params = pltpu.CompilerParams(vmem_limit_bytes=48 * MIB)

    block = min(16, along_local)
    row_shape = jax.ShapeDtypeStruct((row_count, along_local, across_total), jnp.float32)
    row_spec = pl.BlockSpec((row_count, block, across_total), lambda n: (0, n, 0))
    inverse, g_rows, h_rows, spikes = pl.pallas_call(
        spike_kernel,
        grid=(along_local // block,),
        in_specs=[smem] * 4 + [pl.BlockSpec((block, across_total), lambda n: (n, 0))],
        out_specs=[row_spec] * 3
        + [pl.BlockSpec((4, block, across_total), lambda n: (0, n, 0))],
        out_shape=[row_shape] * 3
        + [jax.ShapeDtypeStruct((4, along_local, across_total), jnp.float32)],
        compiler_params=params,
        cost_estimate=pl.CostEstimate(
            flops=12 * row_count * along_local * across_total,
            bytes_accessed=60 * MIB,
            transcendentals=0,
        ),
        name="spikes",
    )(low, up, diag, curve_rows, square)
    all_spikes = lax.all_gather(spikes, "gy")

    block = min(8, along_local)
    full_spec = pl.BlockSpec((row_count, block, modes), lambda n: (0, n, 0))
    half_spec = pl.BlockSpec((row_count, block, across_total), lambda n: (0, n, 0))
    swept, edges = pl.pallas_call(
        functools.partial(sweep_kernel, chunks),
        grid=(along_local // block,),
        in_specs=[smem] * 2
        + [half_spec]
        + [pl.BlockSpec((groups, per_chunk, block, modes), lambda n: (0, 0, n, 0))] * chunks,
        out_specs=[full_spec, pl.BlockSpec((2, block, modes), lambda n: (0, n, 0))],
        out_shape=[
            jax.ShapeDtypeStruct((row_count, along_local, modes), jnp.float32),
            jax.ShapeDtypeStruct((2, along_local, modes), jnp.float32),
        ],
        compiler_params=params,
        name="sweep",
    )(low, up, inverse, *sources)
    all_edges = lax.all_gather(edges, "gy")
    return pl.pallas_call(
        functools.partial(finish_kernel, gy),
        grid=(along_local // block,),
        in_specs=[
            smem, full_spec, half_spec, half_spec,
            pl.BlockSpec((gy, 2, block, modes), lambda n: (0, 0, n, 0)),
            pl.BlockSpec((gy, 4, block, across_total), lambda n: (0, 0, n, 0)),
        ],
        out_specs=pl.BlockSpec((1, row_count, block, modes), lambda n: (0, 0, n, 0)),
        out_shape=jax.ShapeDtypeStruct((1, row_count, along_local, modes), jnp.float32),
        compiler_params=params,
        name="finish",
    )(jnp.reshape(my_group, (1,)).astype(jnp.int32), swept, g_rows, h_rows, all_edges, all_spikes)


def solution(mesh):
    placed = (P(None, "gy", "gz", "gx"), P(), P(), P(), P(), P())

    def run(fields, *rest):
        pieces = two_pieces(across_matrix(fields.shape[2])) + two_pieces(
            along_matrix(fields.shape[3])
        )
        pieces = tuple(jnp.asarray(a) for a in pieces)
        return jax.shard_map(
            local,
            mesh=mesh,
            in_specs=((P(),) * 4,) + placed,
            out_specs=P(None, "gy", ("gx", "gz"), None),
            check_vma=False,
        )(pieces, fields, *rest)

    return run
```
